256 devices in a mesh: shot: 32 (over x_lo, z, core), freq: 8 (over x_hi, y).
Axes of the slice: x: 4 (x_hi: 2, x_lo: 2; x = x_hi * 2 + x_lo), y: 4, z: 8, core: 2. Of those that a mesh axis runs over, the one named last changes fastest.
Arguments:
- wavefield: bfloat16 [2, 16, 4096, 4096], P(None, 'freq', 'shot'), may hold values from -0.75 to 0.75
- wavelet: float32 [2, 16], P(None, 'freq'), may hold values from -3 to 3
- shot_owner: int32 [4096, 1], P('shot'), may hold values from 0 to 31; in each aligned block of 128 rows (0 to 127, 128 to 255, ...) at most 8 rows name the same one
- trace_map: int32 [4096, 512], P('shot'), may hold values from 0 to 511, each once within a row
Outputs:
- multiples: bfloat16 [32, 8192, 512], P('freq', 'shot')
The draws below stay inside these ranges and needn't reach their ends.
Inputs may be any that keep to these rules, and one draw needn't show every extreme that they name: `shot_owner`: among the 128 shots of one device no owner is named more than 8 times, and in some device one owner is named exactly 8 times. `trace_map`: each row is a permutation of the 512 window receivers.
All inputs are finite; a program needn't handle non-finite values.
Results may differ from the reference program's by a relative error of at most 0.017.
Values may be sent and summed in bfloat16 or wider, within the bound.
No kernel may reach another device: no remote copies, remote signals or barrier semaphores. Data moves between devices by JAX's collectives and lax.ppermute only.
A program may use at most 64 MiB of HBM per device.

```python
import math
from functools import partial
import jax
import jax.numpy as jnp
import numpy as np
from jax import lax

S_DEV = 128
R_WIN = 512
SHOTS = 4096
HERTZ_BINS = 16
NT = 32
CAP = 8
N_SHOT = 32


def block_levels(key, extent, cuts, smallest, top_value):
    factor_of = 1.0
    for axis_at, shards_of in cuts:
        heights = jax.random.uniform(jax.random.fold_in(jax.random.fold_in(key, 6), axis_at), (shards_of,), jnp.float32, smallest / len(cuts), top_value / len(cuts))
        factor_of = factor_of * jnp.repeat(jnp.exp(heights), extent[axis_at] // shards_of).reshape((-1,) + (1,) * (len(extent) - 1 - axis_at))
    return factor_of


def assign_block(stream_key, own, number, rows, number_of, top, reach, slope):
    ranking = jax.random.permutation(stream_key, number_of)
    packed, common = shares(number_of, rows * top, reach, slope, True), shares(number_of, rows * top, reach, slope, False)
    places = jnp.arange(number_of)

    def named(lengths, offset_by):
        used = int((lengths > 0).sum())
        fixed = max(1, used // 4)
        shifted = fixed + (places - fixed + offset_by * (used - fixed)) % max(1, number_of - fixed)
        return jnp.zeros((number_of,), jnp.int32).at[ranking[jnp.where(places < fixed, places, shifted)]].set(jnp.asarray(lengths, jnp.int32))

    lengths = jnp.where(number % 4 == 0, named(packed, number // 4), named(common, number - number // 4 - 1))
    mixed = jax.random.permutation(jax.random.fold_in(own, 3), number_of)
    giver, taker = mixed[0:number_of // 2 * 2:2], mixed[1:number_of // 2 * 2:2]
    margin = jnp.minimum(lengths[giver] - 1, reach - lengths[taker]) // 2
    margin = jnp.where((giver == ranking[0]) | (taker == ranking[0]) | (lengths[taker] == 0), 0, jnp.maximum(margin, 0))
    shifted = jax.random.randint(jax.random.fold_in(own, 4), (number_of // 2,), 0, 1 << 20) % (margin + 1)
    lengths = lengths.at[giver].add(-shifted).at[taker].add(shifted)
    members = jnp.searchsorted(jnp.cumsum(lengths), jnp.arange(rows * top), side="right").astype(jnp.int32)
    grid = members.reshape(top, rows).T
    grid = grid[jax.random.permutation(jax.random.fold_in(own, 1), rows)]
    offset_by = jax.random.randint(jax.random.fold_in(own, 2), (rows, 1), 0, top)
    return jnp.take_along_axis(grid, (jnp.arange(top)[None, :] + offset_by) % top, axis=1)


def shares(number_of, total, most, slope, full):
    loads = [(1 << 20) // math.isqrt(standing ** slope) + 1 for standing in range(1, number_of + 1)]
    largest = most if full else min(most, max(-(-total // number_of), total * loads[0] // sum(loads)))
    least = 1 if total - largest >= number_of - 1 else 0
    holding, surplus = [largest] + [least] * (number_of - 1), total - largest - least * (number_of - 1)
    while surplus > 0:
        movable = [i for i in range(1, number_of) if holding[i] < largest] or [i for i in range(1, number_of) if holding[i] < most]
        mass, left = sum([loads[i] for i in movable]), surplus
        for i in movable:
            more = min(most - holding[i], max(1, left * loads[i] // mass), surplus)
            holding[i] = holding[i] + more
            surplus = surplus - more
    return np.array(holding)


def gaussian(key, shape, deviation, most, pieces=(), kind=jnp.bfloat16):
    level = block_levels(key, shape, pieces, -0.22, 0.18) if pieces else 1.0
    values = jax.random.normal(key, shape, jnp.float32) * deviation * level
    return jnp.minimum(jnp.maximum(values, -most), most).astype(kind)


def setup_inputs(seed: int = 0) -> dict:
    key_list = jax.random.split(jax.random.key(seed), 5)
    wavefield = gaussian(key_list[0], (2, HERTZ_BINS, SHOTS, SHOTS), 0.125, 0.75, ((1, 8), (2, 32)))
    wavelet = gaussian(key_list[1], (2, HERTZ_BINS), 1.0, 3.0, ((1, 8),), jnp.float32)
    shot_owner_keys = jax.random.split(jax.random.fold_in(key_list[2], 1), SHOTS // S_DEV)
    shot_owner_turns = jax.random.permutation(jax.random.fold_in(key_list[2], 3), SHOTS // S_DEV)
    shot_owner = jax.vmap(lambda own, number: assign_block(jax.random.fold_in(key_list[2], 2), own, number, S_DEV, N_SHOT, 1, CAP, 2))(shot_owner_keys, shot_owner_turns).reshape((SHOTS, 1))
    trace_map = jax.vmap(lambda own: jax.random.permutation(own, R_WIN))(jax.random.split(key_list[3], SHOTS)).reshape((SHOTS, R_WIN)).astype(jnp.int32)
    return dict(wavefield=wavefield, wavelet=wavelet, shot_owner=shot_owner, trace_map=trace_map)


def wave_tables(time_index, freq_index, freq_total):
    phase_turns = ((freq_index[None, :] + 1) * time_index[:, None]) % (2 * freq_total)
    angles = phase_turns.astype(jnp.float32) * (jnp.pi / freq_total)
    return jnp.cos(angles) / freq_total, jnp.sin(angles) / freq_total


def reference(wavefield, wavelet, shot_owner, trace_map):
    cutoff_hertz_bin = lax.Precision.HIGHEST
    product = partial(jnp.dot, precision=cutoff_hertz_bin)

    def estimate_echoes(slice_index):
        layer_field = lax.dynamic_index_in_dim(wavefield, slice_index, 1, keepdims=False)
        left_real = layer_field[0].astype(jnp.float32)
        left_imag = layer_field[1].astype(jnp.float32)
        right_real = left_real[:, :R_WIN]
        right_imag = left_imag[:, :R_WIN]
        inphase_entry = product(left_real, right_real) - product(left_imag, right_imag)
        quadrature_entry = product(left_real, right_imag) + product(left_imag, right_real)
        inphase_weight = wavelet[0, slice_index]
        quadrature_weight = wavelet[1, slice_index]
        estimate_inphase = (inphase_entry * inphase_weight - quadrature_entry * quadrature_weight).astype(jnp.bfloat16)
        estimate_quadrature = (inphase_entry * quadrature_weight + quadrature_entry * inphase_weight).astype(jnp.bfloat16)
        return estimate_inphase, estimate_quadrature

    estimate_inphase, estimate_quadrature = lax.map(estimate_echoes, jnp.arange(HERTZ_BINS, dtype=jnp.int32))
    estimate_inphase, estimate_quadrature = lax.optimization_barrier((estimate_inphase, estimate_quadrature))
    even_basis_table, odd_basis_table = wave_tables(jnp.arange(NT, dtype=jnp.int32), jnp.arange(HERTZ_BINS, dtype=jnp.int32), HERTZ_BINS)
    recorded_wiggles = jnp.einsum("vq,qjl->vjl", even_basis_table, estimate_inphase.astype(jnp.float32), precision=cutoff_hertz_bin)
    recorded_wiggles = recorded_wiggles - jnp.einsum("vq,qjl->vjl", odd_basis_table, estimate_quadrature.astype(jnp.float32), precision=cutoff_hertz_bin)
    recorded_wiggles = recorded_wiggles.astype(jnp.bfloat16)
    arranged = jnp.take_along_axis(recorded_wiggles, trace_map[None, :, :], axis=2)
    chosen = shot_owner[:, 0]
    owner_marks = (chosen[:, None] == jnp.arange(N_SHOT, dtype=jnp.int32)[None, :]).astype(jnp.int32)
    owner_marks = owner_marks.reshape(N_SHOT, S_DEV, N_SHOT)
    before = jnp.cumsum(owner_marks, axis=1) - owner_marks
    rank_within = jnp.sum(before * owner_marks, axis=2).reshape(SHOTS).astype(jnp.int32)
    source = jnp.arange(SHOTS, dtype=jnp.int32) // S_DEV
    out_rows = chosen * (N_SHOT * CAP) + source * CAP + rank_within
    multiples = jnp.zeros((NT, N_SHOT * N_SHOT * CAP, R_WIN), jnp.bfloat16)
    return multiples.at[:, out_rows, :].set(arranged)
```

```python
import jax
import jax.numpy as jnp
import numpy as np
from jax import lax
from jax.experimental import pallas as pl
from jax.experimental.pallas import tpu as pltpu
from jax.sharding import Mesh, PartitionSpec as P

SHOTS = 128
WINDOW = 512
FREQS = 16
TIMES = 32
SLOTS = 8
OWNERS = 32
PART_SHOTS = 16
SHOT_AXES = ("xl", "z", "core")
FREQ_AXES = ("xh", "y")
BF = jnp.bfloat16
F32 = jnp.float32


def transform_tables():
    f = np.arange(FREQS)[None, :]
    t = np.arange(TIMES)[:, None]
    angle = ((f + 1) * t) % (2 * FREQS) * (np.pi / FREQS)
    table = np.stack([np.cos(angle), -np.sin(angle)], axis=2) / FREQS
    table = table.reshape(TIMES, 2 * FREQS)
    eye = np.eye(PART_SHOTS)
    full = np.einsum("tq,ab->atqb", table, eye)
    full = full.reshape(PART_SHOTS * TIMES, 2 * FREQS * PART_SHOTS).astype(np.float32)
    high = full.astype(BF)
    low = (full - high.astype(np.float32)).astype(BF)
    order = np.einsum("ts,ab->tabs", np.eye(TIMES), eye)
    order = order.reshape(TIMES * PART_SHOTS, PART_SHOTS * TIMES).astype(BF)
    return high, low, order


def convolve_kernel(
    place, wave, a0p, a0q, a1p, a1q, a1w, g1, g1s, g2, g2s, out, acc_r, acc_i
):
    step = pl.program_id(0)
    xl = place[0]
    core = place[1]

    @pl.when(step == 0)
    def _():
        acc_r[...] = jnp.zeros_like(acc_r)
        acc_i[...] = jnp.zeros_like(acc_i)

    def rows(own, other, part):
        mine = own[0, part]
        theirs = other[0, part]
        first = jnp.where(core == 0, mine, theirs)
        second = jnp.where(core == 0, theirs, mine)
        return [first, second]

    def left(block, part, is_own_half):
        column = jnp.where(is_own_half, xl, 1 - xl) * 8 + step
        return jnp.where(column < 2, a1w[part], block[part])

    br = jnp.concatenate(rows(g1, g1s, 0) + rows(g2, g2s, 0), axis=0)
    bi = jnp.concatenate(rows(g1, g1s, 1) + rows(g2, g2s, 1), axis=0)
    ar = jnp.concatenate(
        [
            jnp.concatenate([a0p[0, 0], a0q[0, 0]], axis=1),
            jnp.concatenate([left(a1p, 0, True), left(a1q, 0, False)], axis=1),
        ],
        axis=0,
    )
    ai = jnp.concatenate(
        [
            jnp.concatenate([a0p[1, 0], a0q[1, 0]], axis=1),
            jnp.concatenate([left(a1p, 1, True), left(a1q, 1, False)], axis=1),
        ],
        axis=0,
    )
    dot = lambda a, b: jnp.dot(a, b, preferred_element_type=F32)
    acc_r[...] += dot(ar, br) - dot(ai, bi)
    acc_i[...] += dot(ar, bi) + dot(ai, br)

    @pl.when(step == pl.num_programs(0) - 1)
    def _():
        wr = wave[0, xl]
        wi = wave[1, xl]
        er = (acc_r[...] * wr - acc_i[...] * wi).astype(BF)
        ei = (acc_r[...] * wi + acc_i[...] * wr).astype(BF)
        for block in range(2):
            where = xl if block == 0 else 1 - xl
            for part in range(8):
                first = block * SHOTS + part * PART_SHOTS
                out[2 * part + where, 0:16, :] = er[first : first + 16]
                out[2 * part + where, 16:32, :] = ei[first : first + 16]


def convolve(place, wavelet, wavefield, swapped, swapped_window, g1, g1s, g2, g2s):
    a0 = lambda half: pl.BlockSpec(
        (2, 1, SHOTS, 256),
        lambda k, p: (0, p[0], 0, (p[0] if half == 0 else 1 - p[0]) * 8 + k),
    )
    a1 = lambda half: pl.BlockSpec(
        (2, SHOTS, 256),
        lambda k, p: (0, 0, jnp.maximum((p[0] if half == 0 else 1 - p[0]) * 8 + k - 2, 0)),
    )
    window = pl.BlockSpec((2, SHOTS, 256), lambda k, p: (0, 0, jnp.minimum(k, 1)))
    gathered = pl.BlockSpec((1, 2, SHOTS, WINDOW), lambda k, p: (k, 0, 0, 0))
    return pl.pallas_call(
        convolve_kernel,
        out_shape=jax.ShapeDtypeStruct((16, 32, WINDOW), BF),
        grid_spec=pltpu.PrefetchScalarGridSpec(
            num_scalar_prefetch=1,
            grid=(8,),
            in_specs=[pl.BlockSpec(memory_space=pltpu.SMEM)]
            + [a0(0), a0(1), a1(0), a1(1), window]
            + [gathered] * 4,
            out_specs=pl.BlockSpec((16, 32, WINDOW), lambda k, p: (0, 0, 0)),
            scratch_shapes=[pltpu.VMEM((256, WINDOW), F32)] * 2,
        ),
        compiler_params=pltpu.CompilerParams(
            dimension_semantics=("arbitrary",), vmem_limit_bytes=40 * 1024 * 1024
        ),
        cost_estimate=pl.CostEstimate(
            flops=2 * 256 * 4096 * 512 * 4, bytes_accessed=13 * 2**20, transcendentals=0
        ),
    )(place, wavelet, wavefield, wavefield, swapped, swapped, swapped_window, g1, g1s, g2, g2s)


def transform_kernel(spectra, high, low, order, trace_map, out, traces, moved):
    dot = lambda a, b: jnp.dot(a, b, preferred_element_type=F32)
    x = spectra[...].reshape(512, WINDOW)
    traces[...] = (dot(high[...], x) + dot(low[...], x)).astype(BF)
    receivers = lax.broadcasted_iota(jnp.int32, (WINDOW, WINDOW), 0)
    for shot in range(PART_SHOTS):
        chosen = jnp.where(receivers == trace_map[shot : shot + 1, :], 1.0, 0.0).astype(BF)
        picked = dot(traces[shot * TIMES : (shot + 1) * TIMES, :], chosen)
        moved[shot * TIMES : (shot + 1) * TIMES, :] = picked.astype(BF)
    out[...] = dot(order[...], moved[...]).astype(BF)


def transform(spectra, trace_map):
    high, low, order = transform_tables()
    return pl.pallas_call(
        transform_kernel,
        out_shape=jax.ShapeDtypeStruct((TIMES * PART_SHOTS, WINDOW), BF),
        scratch_shapes=[pltpu.VMEM((512, WINDOW), BF)] * 2,
        compiler_params=pltpu.CompilerParams(vmem_limit_bytes=40 * 1024 * 1024),
    )(spectra, jnp.asarray(high), jnp.asarray(low), jnp.asarray(order), trace_map)


def slot_matrix(owners):
    same = owners[:, None] == owners[None, :]
    position = jnp.arange(SHOTS, dtype=jnp.int32)
    rank = jnp.sum(same & (position[:, None] > position[None, :]), axis=1, dtype=jnp.int32)
    slot = owners * SLOTS + rank
    times = 4
    column = jnp.broadcast_to(slot.reshape(8, 1, PART_SHOTS), (8, times, PART_SHOTS))
    column_time = jnp.arange(times, dtype=jnp.int32)[None, :, None]
    key = ((column // SLOTS) * times + column_time) * SLOTS + column % SLOTS
    row = jnp.arange(OWNERS * times * SLOTS, dtype=jnp.int32)
    return (row[:, None] == key.reshape(1, 512)).astype(BF)


def shards(wavefield, wavelet, shot_owner, trace_map):
    xl = lax.axis_index("xl")
    core = lax.axis_index("core")
    group = lax.axis_index(FREQ_AXES)
    swap = [(0, 1), (1, 0)]
    own = lax.dynamic_slice_in_dim(wavefield[..., :WINDOW], xl, 1, 1)[:, 0]
    give_window = lax.dynamic_slice_in_dim(wavefield[..., :WINDOW], 1 - xl, 1, 1)[:, 0]
    give = lax.dynamic_slice_in_dim(wavefield[..., WINDOW:], 1 - xl, 1, 1)[:, 0]
    swapped_window = lax.ppermute(give_window, "xl", swap)
    g1 = lax.all_gather(own, "z", axis=0)
    swapped = lax.ppermute(give, "xl", swap)
    g2 = lax.all_gather(swapped_window, "z", axis=0)
    g1s = lax.ppermute(g1, "core", swap)
    g2s = lax.ppermute(g2, "core", swap)
    place = jnp.stack([xl, core]).astype(jnp.int32)
    estimate = convolve(
        place, wavelet, wavefield, swapped, swapped_window, g1, g1s, g2, g2s
    )
    spectra = lax.all_to_all(estimate, ("xh", "y", "xl"), 0, 0, tiled=True)
    part_map = lax.dynamic_slice_in_dim(trace_map, group * PART_SHOTS, PART_SHOTS, 0)
    arranged = transform(spectra, part_map)
    times = lax.all_to_all(arranged.reshape(8, 64, WINDOW), FREQ_AXES, 0, 0, tiled=True)
    slots = slot_matrix(shot_owner[:, 0])
    outgoing = jnp.dot(slots, times.reshape(512, WINDOW), preferred_element_type=F32)
    outgoing = outgoing.astype(BF).reshape(OWNERS, 4 * SLOTS, WINDOW)
    arrived = lax.all_to_all(outgoing, SHOT_AXES, 0, 0, tiled=True)
    arrived = arrived.reshape(OWNERS, 4, SLOTS, WINDOW)
    return jnp.transpose(arrived, (1, 0, 2, 3)).reshape(4, OWNERS * SLOTS, WINDOW)


def solution(mesh):
    fine = Mesh(mesh.devices.reshape(2, 8, 2, 2, 4), SHOT_AXES + FREQ_AXES)
    placed = (
        P(None, FREQ_AXES, SHOT_AXES, None),
        P(None, FREQ_AXES),
        P(SHOT_AXES, None),
        P(SHOT_AXES, None),
    )
    return jax.shard_map(
        shards,
        mesh=fine,
        in_specs=placed,
        out_specs=P(FREQ_AXES, SHOT_AXES, None),
        check_vma=False,
    )
```

```python
import jax
import jax.numpy as jnp
import numpy as np
from jax import lax
from jax.experimental import pallas as pl
from jax.experimental.pallas import tpu as pltpu
from jax.sharding import Mesh, PartitionSpec as P

SHOTS = 128
WINDOW = 512
FREQS = 16
TIMES = 32
OWNERS = 32
PART_SHOTS = 16
DEPTH = 8
SHOT_AXES = ("xl", "z", "core")
FREQ_AXES = ("xh", "y")
BF = jnp.bfloat16
F32 = jnp.float32
PARAMS = pltpu.CompilerParams(vmem_limit_bytes=48 * 1024 * 1024)


def dot(a, b):
    return jnp.dot(a, b, preferred_element_type=F32)


def transform_tables():
    f = np.arange(FREQS)[None, :]
    t = np.arange(TIMES)[:, None]
    angle = ((f + 1) * t) % (2 * FREQS) * (np.pi / FREQS)
    table = np.stack([np.cos(angle), -np.sin(angle)], axis=2) / FREQS
    table = table.reshape(TIMES, 2 * FREQS)
    full = np.einsum("tq,ab->atqb", table, np.eye(PART_SHOTS))
    full = full.reshape(PART_SHOTS * TIMES, 2 * FREQS * PART_SHOTS).astype(np.float32)
    high = full.astype(BF)
    low = (full - high.astype(np.float32)).astype(BF)
    return high, low


HBM = pl.BlockSpec(memory_space=pltpu.HBM)
ANY = pl.BlockSpec(memory_space=pl.ANY)
SMEM = pl.BlockSpec(memory_space=pltpu.SMEM)
CHUNK = 1024
STRIP = 16


def run_copies(pairs, sems):
    copies = [
        pltpu.make_async_copy(source, target, sems.at[n])
        for n, (source, target) in enumerate(pairs)
    ]
    for copy in copies:
        copy.start()
    return copies


def window_kernel(place, wave, strip, own, give, sems):
    pairs = []
    for target, freq in ((own, place[0]), (give, 1 - place[0])):
        for part in range(2):
            for column in range(4):
                pairs.append(
                    (
                        wave.at[part, freq, :, pl.ds(column * 128, 128)],
                        target.at[pl.ds((part * 4 + column) * 128, 128), :],
                    )
                )
        pairs.append((strip, target.at[pl.ds(CHUNK, STRIP), :]))
    for copy in run_copies(pairs, sems):
        copy.wait()


def window_chunks(place, wavefield, strip):
    return pl.pallas_call(
        window_kernel,
        out_shape=[jax.ShapeDtypeStruct((CHUNK + STRIP, 128), BF)] * 2,
        in_specs=[SMEM, HBM, ANY],
        out_specs=[ANY] * 2,
        scratch_shapes=[pltpu.SemaphoreType.DMA((18,))],
        compiler_params=PARAMS,
    )(place, wavefield, strip)


def halves_kernel(place, wave, diag, same, partner, far, near, sems):
    xl, core = place[0], place[1]
    copies = run_copies(
        [
            (wave.at[0, 1 - xl, :, pl.ds(WINDOW, 3584)], far.at[0]),
            (wave.at[1, 1 - xl, :, pl.ds(WINDOW, 3584)], far.at[1]),
            (wave.at[0, xl], near.at[0]),
            (wave.at[1, xl], near.at[1]),
        ],
        sems,
    )
    for n, copy in enumerate(copies):
        copy.wait()
        part = n % 2
        here = far if n < 2 else near
        for block in range(14 if n < 2 else 16):
            a = here[part, :, block * 256 : block * 256 + 128]
            b = here[part, :, block * 256 + 128 : block * 256 + 256]
            target = slice(block * 128, block * 128 + 128)
            if n < 2:
                same[part, :, target] = jnp.where(core == 0, a, b)
                diag[part, :, target] = jnp.where(core == 0, b, a)
            else:
                partner[part, :, target] = jnp.where(core == 0, b, a)


def column_halves(place, wavefield):
    return pl.pallas_call(
        halves_kernel,
        out_shape=[
            jax.ShapeDtypeStruct((2, SHOTS, 1792), BF),
            jax.ShapeDtypeStruct((2, SHOTS, 1792), BF),
            jax.ShapeDtypeStruct((2, SHOTS, 2048), BF),
        ],
        in_specs=[SMEM, HBM],
        scratch_shapes=[
            pltpu.VMEM((2, SHOTS, 3584), BF),
            pltpu.VMEM((2, SHOTS, 4096), BF),
            pltpu.SemaphoreType.DMA((4,)),
        ],
        compiler_params=PARAMS,
    )(place, wavefield)


def follow_kernel(value, earlier, out):
    pass


def follow(value, earlier, flops=0):
    return pl.pallas_call(
        follow_kernel,
        cost_estimate=pl.CostEstimate(flops=flops, bytes_accessed=flops // 500, transcendentals=0),
        out_shape=jax.ShapeDtypeStruct(value.shape, value.dtype),
        in_specs=[pl.BlockSpec(memory_space=pl.ANY)] * 2,
        out_specs=pl.BlockSpec(memory_space=pl.ANY),
        input_output_aliases={0: 0},
    )(value, earlier)


def pick(place, block, refs, part):
    if len(refs) == 1:
        return refs[0][part, :, pl.ds(pl.multiple_of(block * 128, 128), 128)]
    rest, window = refs
    late = jnp.maximum(block - 2, 0)
    early = jnp.minimum(block, 1) * 2 + place[1]
    a = rest[part, :, pl.ds(pl.multiple_of(late * 128, 128), 128)]
    b = window[pl.ds(pl.multiple_of((part * 4 + early) * 128, 128), 128), :]
    return jnp.where(block < 2, b, a)


def window_columns(chunk, part):
    return jnp.concatenate(
        [chunk[(part * 4 + n) * 128 : (part * 4 + n + 1) * 128, :] for n in range(4)], axis=1
    )


def multiply(place, rows, near, far, depth):
    xl = place[0]
    sides = []
    for part in range(2):
        lines = []
        for refs in rows:
            a = pick(place, xl * DEPTH + depth, refs, part)
            b = pick(place, (1 - xl) * DEPTH + depth, refs, part)
            lines.append(jnp.concatenate([a, b], axis=1))
        sides.append(jnp.concatenate(lines, axis=0))
    ar, ai = sides
    lines = jnp.concatenate([ar, -ai], axis=1), jnp.concatenate([ai, ar], axis=1)
    columns = [window_columns(chunk, part) for part in range(2) for chunk in (near, far)]
    return dot(jnp.concatenate(lines, axis=0), jnp.concatenate(columns, axis=0))


def product(place, wavefield, line, other_line, near, far):
    distances = list(far)
    count = len(distances)
    size = 2 * SHOTS
    rest, window = other_line

    def kernel(place, line_in, rest_in, window_in, *refs):
        near_in, far_in = refs[:count], refs[count : 2 * count]
        out, total, near_here, far_here, line_here, rest_here, window_here, sems = refs[2 * count :]
        pairs = [(rest_in, rest_here), (window_in.at[pl.ds(0, CHUNK), :], window_here)]
        if line is None:
            for block in range(16):
                column = pl.multiple_of((2 * block + place[1]) * 128, 128)
                pairs.append(
                    (
                        line_in.at[:, place[0], :, pl.ds(column, 128)],
                        line_here.at[:, :, pl.ds(block * 128, 128)],
                    )
                )
        else:
            pairs.append((line_in, line_here))
        first = len(pairs)
        for n in range(count):
            pairs.append((near_in[n].at[pl.ds(0, CHUNK), :], near_here.at[n]))
            pairs.append((far_in[n].at[pl.ds(0, CHUNK), :], far_here.at[n]))
        copies = run_copies(pairs, sems)
        for copy in copies[:first]:
            copy.wait()
        groups = [(line_here,), (rest_here, window_here)]
        for n in range(count):
            copies[first + 2 * n].wait()
            copies[first + 2 * n + 1].wait()
            depth = lax.rem(place[2] - distances[n] + 2 * DEPTH, DEPTH)
            value = multiply(place, groups, near_here.at[n], far_here.at[n], depth)
            if n == 0:
                total[...] = value
            elif n < count - 1:
                total[...] += value
            else:
                out[0] = total[:size] + value[:size]
                out[1] = total[size:] + value[size:]

    return pl.pallas_call(
        kernel,
        out_shape=jax.ShapeDtypeStruct((2, size, WINDOW), F32),
        in_specs=[SMEM, HBM if line is None else ANY] + [ANY] * (2 + 2 * count),
        scratch_shapes=[
            pltpu.VMEM((2 * size, WINDOW), F32),
            pltpu.VMEM((count, CHUNK, 128), BF),
            pltpu.VMEM((count, CHUNK, 128), BF),
            pltpu.VMEM((2, SHOTS, 2048), BF),
            pltpu.VMEM(rest.shape, BF),
            pltpu.VMEM((CHUNK, 128), BF),
            pltpu.SemaphoreType.DMA((18 + 2 * count,)),
        ],
        compiler_params=PARAMS,
        cost_estimate=pl.CostEstimate(
            flops=2 * size * 512 * 1024 * count, bytes_accessed=2**22, transcendentals=0
        ),
    )(
        place,
        wavefield if line is None else line,
        rest,
        window,
        *[near[d] for d in distances],
        *[far[d] for d in distances],
    )


def scale_kernel(place, wave, keep, came, order_own, order_other, out):
    xl = place[0]
    wr = wave[0, xl]
    wi = wave[1, xl]
    for block in range(2):
        where = xl if block == 0 else 1 - xl
        order = order_own[...] if block == 0 else order_other[...]
        rows = slice(block * SHOTS, (block + 1) * SHOTS)
        real = keep[0, rows] + came[0, rows]
        imag = keep[1, rows] + came[1, rows]
        er = (real * wr - imag * wi).astype(BF)
        ei = (real * wi + imag * wr).astype(BF)
        sr = dot(order, er).astype(BF)
        si = dot(order, ei).astype(BF)
        for part in range(8):
            some = slice(part * PART_SHOTS, (part + 1) * PART_SHOTS)
            out[2 * part + where, 0:16, :] = sr[some]
            out[2 * part + where, 16:32, :] = si[some]


def scale(place, wavelet, keep, came, order_own, order_other):
    return pl.pallas_call(
        scale_kernel,
        out_shape=jax.ShapeDtypeStruct((16, 32, WINDOW), BF),
        in_specs=[pl.BlockSpec(memory_space=pltpu.SMEM)] * 2
        + [pl.BlockSpec(memory_space=pltpu.VMEM)] * 4,
        compiler_params=PARAMS,
    )(place, wavelet, keep, came, order_own, order_other)


def transform_kernel(spectra, high, low, trace_map, spread, swapped, out, traces, moved):
    x = spectra[...].reshape(512, WINDOW)
    traces[...] = (dot(high[...], x) + dot(low[...], x)).astype(BF)
    receivers = lax.broadcasted_iota(jnp.int32, (WINDOW, WINDOW), 0)
    for shot in range(PART_SHOTS):
        rows = slice(shot * TIMES, (shot + 1) * TIMES)
        chosen = jnp.where(receivers == trace_map[shot : shot + 1, :], 1.0, 0.0).astype(BF)
        moved[rows, :] = dot(traces[rows, :], chosen).astype(BF)
    upper = lax.broadcasted_iota(jnp.int32, (128, 8, 128), 1) < 4
    even, odd = [], []
    for pair in range(2):
        first = slice(pair * 256, pair * 256 + 128)
        second = slice(pair * 256 + 128, pair * 256 + 256)
        both = moved[:, pair * 256 : (pair + 1) * 256]
        plain = dot(spread[...], both).reshape(128, 8, 256)
        other = dot(swapped[...], both).reshape(128, 8, 256)
        even.append(jnp.where(upper, plain[..., :128], other[..., 128:]))
        odd.append(jnp.where(upper, other[..., :128], plain[..., 128:]))
    out[:, 0] = jnp.concatenate(even, axis=1).astype(BF)
    out[:, 1] = jnp.concatenate(odd, axis=1).astype(BF)


def transform(spectra, trace_map, spread, swapped):
    high, low = transform_tables()
    return pl.pallas_call(
        transform_kernel,
        out_shape=jax.ShapeDtypeStruct((128, 2, 16, 128), BF),
        scratch_shapes=[pltpu.VMEM((512, WINDOW), BF)] * 2,
        compiler_params=PARAMS,
    )(spectra, jnp.asarray(high), jnp.asarray(low), trace_map, spread, swapped)


def place_kernel(arrived, turns, out):
    for pair in range(16):
        block = arrived[pair * 16 : (pair + 1) * 16].reshape(256, 128)
        turned = dot(turns[pair], block).astype(BF)
        for column in range(4):
            for time in range(4):
                first = (column * 4 + time) * 16
                out[time, pair * 16 : (pair + 1) * 16, column * 128 : (column + 1) * 128] = (
                    turned[first : first + 16]
                )


def place_rows(arrived, turns):
    return pl.pallas_call(
        place_kernel,
        out_shape=jax.ShapeDtypeStruct((4, OWNERS * 8, WINDOW), BF),
        compiler_params=PARAMS,
    )(arrived, turns)


def sorted_positions(owners):
    shot = jnp.arange(SHOTS, dtype=jnp.int32)
    less = owners[None, :] < owners[:, None]
    same = (owners[None, :] == owners[:, None]) & (shot[None, :] < shot[:, None])
    return jnp.sum((less | same).astype(jnp.int32), axis=1)


def deal_order(position):
    row = jnp.arange(SHOTS, dtype=jnp.int32)
    wanted = (row % PART_SHOTS) * 8 + row // PART_SHOTS
    return (wanted[:, None] == position[None, :]).astype(BF)


def turn_matrices(near_owners, sources, me):
    number = jnp.arange(OWNERS, dtype=jnp.int32)
    before = jnp.sum((near_owners < me).astype(jnp.int32), axis=1)
    start = jnp.sum(
        jnp.where(number[:, None] == sources[None, :], before[None, :], 0), axis=1
    )
    group = jnp.arange(8, dtype=jnp.int32)
    rank = (group[None, :] - start[:, None] + SHOTS) % 8
    rank = rank.reshape(16, 2, 8, 1, 1)
    source = jnp.arange(2, dtype=jnp.int32).reshape(1, 2, 1, 1, 1)
    column = jnp.arange(4, dtype=jnp.int32).reshape(1, 1, 1, 4, 1)
    time = jnp.arange(4, dtype=jnp.int32).reshape(1, 1, 1, 1, 4)
    key = (column * 64 + time * 16 + source * 8 + rank).reshape(16, 1, 256)
    return (jnp.arange(256, dtype=jnp.int32)[None, :, None] == key).astype(BF)


def shards(wavefield, wavelet, shot_owner, trace_map):
    xl = lax.axis_index("xl")
    core = lax.axis_index("core")
    depth = lax.axis_index("z")
    group = lax.axis_index(FREQ_AXES)
    me = lax.axis_index(SHOT_AXES)
    swap = [(0, 1), (1, 0)]
    cross = [(n, 3 - n) for n in range(4)]
    right = [(n, (n + 1) % DEPTH) for n in range(DEPTH)]
    left = [(n, (n - 1) % DEPTH) for n in range(DEPTH)]
    place = jnp.stack([xl, core, depth]).astype(jnp.int32)

    owners = shot_owner[:, 0]
    strip = jnp.broadcast_to(owners.astype(BF)[None], (STRIP, SHOTS))
    own_window, give_window = window_chunks(place, wavefield, strip)
    xw = lax.ppermute(give_window, "xl", swap)
    diag, same, partner = column_halves(place, wavefield)
    diag = lax.ppermute(diag, ("xl", "core"), cross)
    partner = lax.ppermute(partner, "core", swap)
    same = lax.ppermute(follow(same, diag, 3 * 10**10), "xl", swap)
    xpw = lax.ppermute(xw, "core", swap)
    near = {0: own_window}
    far = {0: xw}
    for step in range(1, 5):
        near[step] = lax.ppermute(near[step - 1], "z", right)
        far[-step] = lax.ppermute(far[1 - step], "z", left)
        if step < 4:
            near[-step] = lax.ppermute(near[1 - step], "z", left)
            far[step] = lax.ppermute(far[step - 1], "z", right)
    far[4] = far.pop(-4)
    send = product(place, wavefield, partner, (diag, xpw), near, far)
    came = lax.ppermute(send, "core", swap)
    keep = product(place, wavefield, None, (same, xw), near, far)

    other_owners = xw[CHUNK].astype(jnp.int32)
    distances = list(far)
    strips = [near[d][CHUNK : CHUNK + 1] for d in distances]
    strips += [far[d][CHUNK : CHUNK + 1] for d in distances]
    strips = jnp.concatenate(strips, axis=0)
    near_owners = jnp.concatenate([strips, lax.ppermute(strips, "core", swap)], axis=0)
    near_owners = near_owners.astype(jnp.int32)
    depths = (depth - jnp.asarray(distances, dtype=jnp.int32) + DEPTH) % DEPTH * 2
    sources = jnp.concatenate([depths + 16 * xl, depths + 16 * (1 - xl)])
    sources = jnp.concatenate([sources + core, sources + 1 - core])
    position = sorted_positions(owners)
    order_own = deal_order(position)
    order_other = deal_order(sorted_positions(other_owners))
    wanted = jnp.arange(PART_SHOTS, dtype=jnp.int32) * 8 + group
    mine = wanted[:, None] == position[None, :]
    part_map = jnp.sum(jnp.where(mine[:, :, None], trace_map[None], 0), axis=1)
    part_owner = jnp.sum(jnp.where(mine, owners[None, :], 0), axis=1)
    key = part_owner[:, None] * TIMES + jnp.arange(TIMES, dtype=jnp.int32)[None, :]
    key = key.reshape(1, PART_SHOTS * TIMES)
    line = jnp.arange(OWNERS * TIMES, dtype=jnp.int32)[:, None]
    spread = (line == key).astype(BF)
    swapped = (line == key + 4 - 8 * ((key // 4) % 2)).astype(BF)

    estimate = scale(place, wavelet, keep, came, order_own, order_other)
    spectra = lax.all_to_all(estimate, FREQ_AXES + ("xl",), 0, 0, tiled=True)
    turns = turn_matrices(near_owners, sources, me)
    rows = transform(spectra, part_map, spread, swapped).reshape(256, 16, 128)
    arrived = lax.all_to_all(rows, SHOT_AXES + FREQ_AXES, 0, 0, tiled=True)
    return place_rows(arrived, turns)


def solution(mesh):
    fine = Mesh(mesh.devices.reshape(2, 8, 2, 2, 4), SHOT_AXES + FREQ_AXES)
    placed = (
        P(None, FREQ_AXES, SHOT_AXES, None),
        P(None, FREQ_AXES),
        P(SHOT_AXES, None),
        P(SHOT_AXES, None),
    )
    return jax.shard_map(
        shards,
        mesh=fine,
        in_specs=placed,
        out_specs=P(FREQ_AXES, SHOT_AXES, None),
        check_vma=False,
    )
```

```python
import jax
import jax.numpy as jnp
import numpy as np
from jax import lax
from jax.experimental import pallas as pl
from jax.experimental.pallas import tpu as pltpu
from jax.sharding import Mesh, PartitionSpec as P

SHOTS = 128
WINDOW = 512
FREQS = 16
TIMES = 32
OWNERS = 32
PART_SHOTS = 16
DEPTH = 8
SHOT_AXES = ("xl", "z", "core")
FREQ_AXES = ("xh", "y")
BF = jnp.bfloat16
F32 = jnp.float32
PARAMS = pltpu.CompilerParams(vmem_limit_bytes=48 * 1024 * 1024)


def dot(a, b):
    return jnp.dot(a, b, preferred_element_type=F32)


def transform_tables():
    f = np.arange(FREQS)[None, :]
    t = np.arange(TIMES)[:, None]
    angle = ((f + 1) * t) % (2 * FREQS) * (np.pi / FREQS)
    table = np.stack([np.cos(angle), -np.sin(angle)], axis=2) / FREQS
    table = table.reshape(TIMES, 2 * FREQS)
    full = np.einsum("tq,ab->atqb", table, np.eye(PART_SHOTS))
    full = full.reshape(PART_SHOTS * TIMES, 2 * FREQS * PART_SHOTS).astype(np.float32)
    high = full.astype(BF)
    low = (full - high.astype(np.float32)).astype(BF)
    return np.concatenate([high, low], axis=0)


HBM = pl.BlockSpec(memory_space=pltpu.HBM)
ANY = pl.BlockSpec(memory_space=pl.ANY)
SMEM = pl.BlockSpec(memory_space=pltpu.SMEM)
CHUNK = 1024
STRIP = 16


def run_copies(pairs, sems):
    copies = [
        pltpu.make_async_copy(source, target, sems.at[n])
        for n, (source, target) in enumerate(pairs)
    ]
    for copy in copies:
        copy.start()
    return copies


def window_kernel(place, wave, strip, own, give, sems):
    pairs = []
    for target, freq in ((own, place[0]), (give, 1 - place[0])):
        for part in range(2):
            for column in range(4):
                pairs.append(
                    (
                        wave.at[part, freq, :, pl.ds(column * 128, 128)],
                        target.at[pl.ds((part * 4 + column) * 128, 128), :],
                    )
                )
        pairs.append((strip, target.at[pl.ds(CHUNK, STRIP), :]))
    for copy in run_copies(pairs, sems):
        copy.wait()


def window_chunks(place, wavefield, strip):
    return pl.pallas_call(
        window_kernel,
        out_shape=[jax.ShapeDtypeStruct((CHUNK + STRIP, 128), BF)] * 2,
        in_specs=[SMEM, HBM, ANY],
        out_specs=[ANY] * 2,
        scratch_shapes=[pltpu.SemaphoreType.DMA((18,))],
        compiler_params=PARAMS,
    )(place, wavefield, strip)


def halves_kernel(place, wave, diag, same, partner, far, near, sems):
    xl, core = place[0], place[1]
    copies = run_copies(
        [
            (wave.at[0, 1 - xl, :, pl.ds(WINDOW, 3584)], far.at[0]),
            (wave.at[1, 1 - xl, :, pl.ds(WINDOW, 3584)], far.at[1]),
            (wave.at[0, xl], near.at[0]),
            (wave.at[1, xl], near.at[1]),
        ],
        sems,
    )
    for n, copy in enumerate(copies):
        copy.wait()
        part = n % 2
        here = far if n < 2 else near
        for block in range(14 if n < 2 else 16):
            a = here[part, :, block * 256 : block * 256 + 128]
            b = here[part, :, block * 256 + 128 : block * 256 + 256]
            target = slice(block * 128, block * 128 + 128)
            if n < 2:
                same[part, :, target] = jnp.where(core == 0, a, b)
                diag[part, :, target] = jnp.where(core == 0, b, a)
            else:
                partner[part, :, target] = jnp.where(core == 0, b, a)


def column_halves(place, wavefield):
    return pl.pallas_call(
        halves_kernel,
        out_shape=[
            jax.ShapeDtypeStruct((2, SHOTS, 1792), BF),
            jax.ShapeDtypeStruct((2, SHOTS, 1792), BF),
            jax.ShapeDtypeStruct((2, SHOTS, 2048), BF),
        ],
        in_specs=[SMEM, HBM],
        scratch_shapes=[
            pltpu.VMEM((2, SHOTS, 3584), BF),
            pltpu.VMEM((2, SHOTS, 4096), BF),
            pltpu.SemaphoreType.DMA((4,)),
        ],
        compiler_params=PARAMS,
    )(place, wavefield)


def follow_kernel(value, earlier, out):
    pass


def follow(value, earlier, flops=0):
    return pl.pallas_call(
        follow_kernel,
        cost_estimate=pl.CostEstimate(flops=flops, bytes_accessed=flops // 500, transcendentals=0),
        out_shape=jax.ShapeDtypeStruct(value.shape, value.dtype),
        in_specs=[pl.BlockSpec(memory_space=pl.ANY)] * 2,
        out_specs=pl.BlockSpec(memory_space=pl.ANY),
        input_output_aliases={0: 0},
    )(value, earlier)


def pick(place, block, refs, part):
    if len(refs) == 1:
        return refs[0][part, :, pl.ds(pl.multiple_of(block * 128, 128), 128)]
    rest, window = refs
    late = jnp.maximum(block - 2, 0)
    early = jnp.minimum(block, 1) * 2 + place[1]
    a = rest[part, :, pl.ds(pl.multiple_of(late * 128, 128), 128)]
    b = window[pl.ds(pl.multiple_of((part * 4 + early) * 128, 128), 128), :]
    return jnp.where(block < 2, b, a)


def window_columns(chunk, part):
    return jnp.concatenate(
        [chunk[(part * 4 + n) * 128 : (part * 4 + n + 1) * 128, :] for n in range(4)], axis=1
    )


def multiply(place, rows, near, far, depth):
    xl = place[0]
    sides = []
    for part in range(2):
        lines = []
        for refs in rows:
            a = pick(place, xl * DEPTH + depth, refs, part)
            b = pick(place, (1 - xl) * DEPTH + depth, refs, part)
            lines.append(jnp.concatenate([a, b], axis=1))
        sides.append(jnp.concatenate(lines, axis=0))
    ar, ai = sides
    lines = jnp.concatenate([ar, -ai], axis=1), jnp.concatenate([ai, ar], axis=1)
    columns = [window_columns(chunk, part) for part in range(2) for chunk in (near, far)]
    return dot(jnp.concatenate(lines, axis=0), jnp.concatenate(columns, axis=0))


def product(place, wavefield, line, other_line, near, far):
    distances = list(far)
    count = len(distances)
    size = 2 * SHOTS
    rest, window = other_line

    def kernel(place, line_in, rest_in, window_in, *refs):
        near_in, far_in = refs[:count], refs[count : 2 * count]
        out, total, near_here, far_here, line_here, rest_here, window_here, sems = refs[2 * count :]
        pairs = [(rest_in, rest_here), (window_in.at[pl.ds(0, CHUNK), :], window_here)]
        if line is None:
            for block in range(16):
                column = pl.multiple_of((2 * block + place[1]) * 128, 128)
                pairs.append(
                    (
                        line_in.at[:, place[0], :, pl.ds(column, 128)],
                        line_here.at[:, :, pl.ds(block * 128, 128)],
                    )
                )
        else:
            pairs.append((line_in, line_here))
        first = len(pairs)
        for n in range(count):
            pairs.append((near_in[n].at[pl.ds(0, CHUNK), :], near_here.at[n]))
            pairs.append((far_in[n].at[pl.ds(0, CHUNK), :], far_here.at[n]))
        copies = run_copies(pairs, sems)
        for copy in copies[:first]:
            copy.wait()
        groups = [(line_here,), (rest_here, window_here)]
        for n in range(count):
            copies[first + 2 * n].wait()
            copies[first + 2 * n + 1].wait()
            depth = lax.rem(place[2] - distances[n] + 2 * DEPTH, DEPTH)
            value = multiply(place, groups, near_here.at[n], far_here.at[n], depth)
            if n == 0:
                total[...] = value
            elif n < count - 1:
                total[...] += value
            else:
                out[0] = total[:size] + value[:size]
                out[1] = total[size:] + value[size:]

    return pl.pallas_call(
        kernel,
        out_shape=jax.ShapeDtypeStruct((2, size, WINDOW), F32),
        in_specs=[SMEM, HBM if line is None else ANY] + [ANY] * (2 + 2 * count),
        scratch_shapes=[
            pltpu.VMEM((2 * size, WINDOW), F32),
            pltpu.VMEM((count, CHUNK, 128), BF),
            pltpu.VMEM((count, CHUNK, 128), BF),
            pltpu.VMEM((2, SHOTS, 2048), BF),
            pltpu.VMEM(rest.shape, BF),
            pltpu.VMEM((CHUNK, 128), BF),
            pltpu.SemaphoreType.DMA((18 + 2 * count,)),
        ],
        compiler_params=PARAMS,
        cost_estimate=pl.CostEstimate(
            flops=2 * size * 512 * 1024 * count, bytes_accessed=2**22, transcendentals=0
        ),
    )(
        place,
        wavefield if line is None else line,
        rest,
        window,
        *[near[d] for d in distances],
        *[far[d] for d in distances],
    )


def scale_kernel(place, wave, keep, came, order_own, order_other, out):
    xl = place[0]
    wr = wave[0, xl]
    wi = wave[1, xl]
    for block in range(2):
        where = xl if block == 0 else 1 - xl
        order = order_own[...] if block == 0 else order_other[...]
        rows = slice(block * SHOTS, (block + 1) * SHOTS)
        real = keep[0, rows] + came[0, rows]
        imag = keep[1, rows] + came[1, rows]
        er = (real * wr - imag * wi).astype(BF)
        ei = (real * wi + imag * wr).astype(BF)
        sr = dot(order, er).astype(BF)
        si = dot(order, ei).astype(BF)
        for part in range(8):
            some = slice(part * PART_SHOTS, (part + 1) * PART_SHOTS)
            out[2 * part + where, 0:16, :] = sr[some]
            out[2 * part + where, 16:32, :] = si[some]


def scale(place, wavelet, keep, came, order_own, order_other):
    return pl.pallas_call(
        scale_kernel,
        out_shape=jax.ShapeDtypeStruct((16, 32, WINDOW), BF),
        in_specs=[pl.BlockSpec(memory_space=pltpu.SMEM)] * 2
        + [pl.BlockSpec(memory_space=pltpu.VMEM)] * 4,
        compiler_params=PARAMS,
    )(place, wavelet, keep, came, order_own, order_other)


def transform_kernel(spectra, tables, trace_map, spread, swapped, out, traces, moved):
    x = spectra[...].reshape(512, WINDOW)
    both = dot(tables[...], x)
    traces[...] = (both[:512] + both[512:]).astype(BF)
    receivers = lax.broadcasted_iota(jnp.int32, (WINDOW, WINDOW), 0)
    for shot in range(PART_SHOTS):
        rows = slice(shot * TIMES, (shot + 1) * TIMES)
        chosen = jnp.where(receivers == trace_map[shot : shot + 1, :], 1.0, 0.0).astype(BF)
        moved[rows, :] = dot(traces[rows, :], chosen).astype(BF)
    upper = lax.broadcasted_iota(jnp.int32, (128, 8, 128), 1) < 4
    even, odd = [], []
    for pair in range(2):
        first = slice(pair * 256, pair * 256 + 128)
        second = slice(pair * 256 + 128, pair * 256 + 256)
        both = moved[:, pair * 256 : (pair + 1) * 256]
        plain = dot(spread[...], both).reshape(128, 8, 256)
        other = dot(swapped[...], both).reshape(128, 8, 256)
        even.append(jnp.where(upper, plain[..., :128], other[..., 128:]))
        odd.append(jnp.where(upper, other[..., :128], plain[..., 128:]))
    out[:, 0] = jnp.concatenate(even, axis=1).astype(BF)
    out[:, 1] = jnp.concatenate(odd, axis=1).astype(BF)


def transform(spectra, trace_map, spread, swapped):
    return pl.pallas_call(
        transform_kernel,
        out_shape=jax.ShapeDtypeStruct((128, 2, 16, 128), BF),
        scratch_shapes=[pltpu.VMEM((512, WINDOW), BF)] * 2,
        compiler_params=PARAMS,
    )(spectra, jnp.asarray(transform_tables()), trace_map, spread, swapped)


def place_kernel(arrived, turns, out):
    for pair in range(16):
        block = arrived[pair * 16 : (pair + 1) * 16].reshape(256, 128)
        turned = dot(turns[pair], block).astype(BF)
        for column in range(4):
            for time in range(4):
                first = (column * 4 + time) * 16
                out[time, pair * 16 : (pair + 1) * 16, column * 128 : (column + 1) * 128] = (
                    turned[first : first + 16]
                )


def place_rows(arrived, turns):
    return pl.pallas_call(
        place_kernel,
        out_shape=jax.ShapeDtypeStruct((4, OWNERS * 8, WINDOW), BF),
        compiler_params=PARAMS,
    )(arrived, turns)


def sorted_positions(owners):
    shot = jnp.arange(SHOTS, dtype=jnp.int32)
    less = owners[None, :] < owners[:, None]
    same = (owners[None, :] == owners[:, None]) & (shot[None, :] < shot[:, None])
    return jnp.sum((less | same).astype(jnp.int32), axis=1)


def deal_order(position):
    row = jnp.arange(SHOTS, dtype=jnp.int32)
    wanted = (row % PART_SHOTS) * 8 + row // PART_SHOTS
    return (wanted[:, None] == position[None, :]).astype(BF)


def turn_matrices(near_owners, sources, me):
    number = jnp.arange(OWNERS, dtype=jnp.int32)
    before = jnp.sum((near_owners < me).astype(jnp.int32), axis=1)
    start = jnp.sum(
        jnp.where(number[:, None] == sources[None, :], before[None, :], 0), axis=1
    )
    group = jnp.arange(8, dtype=jnp.int32)
    rank = (group[None, :] - start[:, None] + SHOTS) % 8
    rank = rank.reshape(16, 2, 8, 1, 1)
    source = jnp.arange(2, dtype=jnp.int32).reshape(1, 2, 1, 1, 1)
    column = jnp.arange(4, dtype=jnp.int32).reshape(1, 1, 1, 4, 1)
    time = jnp.arange(4, dtype=jnp.int32).reshape(1, 1, 1, 1, 4)
    key = (column * 64 + time * 16 + source * 8 + rank).reshape(16, 1, 256)
    return (jnp.arange(256, dtype=jnp.int32)[None, :, None] == key).astype(BF)


def shards(wavefield, wavelet, shot_owner, trace_map):
    xl = lax.axis_index("xl")
    core = lax.axis_index("core")
    depth = lax.axis_index("z")
    group = lax.axis_index(FREQ_AXES)
    me = lax.axis_index(SHOT_AXES)
    swap = [(0, 1), (1, 0)]
    cross = [(n, 3 - n) for n in range(4)]
    right = [(n, (n + 1) % DEPTH) for n in range(DEPTH)]
    left = [(n, (n - 1) % DEPTH) for n in range(DEPTH)]
    place = jnp.stack([xl, core, depth]).astype(jnp.int32)

    owners = shot_owner[:, 0]
    strip = jnp.broadcast_to(owners.astype(BF)[None], (STRIP, SHOTS))
    own_window, give_window = window_chunks(place, wavefield, strip)
    xw = lax.ppermute(give_window, "xl", swap)
    diag, same, partner = column_halves(place, wavefield)
    diag = lax.ppermute(diag, ("xl", "core"), cross)
    partner = lax.ppermute(partner, "core", swap)
    same = lax.ppermute(follow(same, diag, 3 * 10**10), "xl", swap)
    xpw = lax.ppermute(xw, "core", swap)
    near = {0: own_window}
    far = {0: xw}
    for step in range(1, 5):
        near[step] = lax.ppermute(near[step - 1], "z", right)
        far[-step] = lax.ppermute(far[1 - step], "z", left)
        if step < 4:
            near[-step] = lax.ppermute(near[1 - step], "z", left)
            far[step] = lax.ppermute(far[step - 1], "z", right)
    far[4] = far.pop(-4)
    send = product(place, wavefield, partner, (diag, xpw), near, far)
    came = lax.ppermute(send, "core", swap)
    keep = product(place, wavefield, None, (same, xw), near, far)

    other_owners = xw[CHUNK].astype(jnp.int32)
    distances = list(far)
    strips = [near[d][CHUNK : CHUNK + 1] for d in distances]
    strips += [far[d][CHUNK : CHUNK + 1] for d in distances]
    strips = jnp.concatenate(strips, axis=0)
    near_owners = jnp.concatenate([strips, lax.ppermute(strips, "core", swap)], axis=0)
    near_owners = near_owners.astype(jnp.int32)
    depths = (depth - jnp.asarray(distances, dtype=jnp.int32) + DEPTH) % DEPTH * 2
    sources = jnp.concatenate([depths + 16 * xl, depths + 16 * (1 - xl)])
    sources = jnp.concatenate([sources + core, sources + 1 - core])
    position = sorted_positions(owners)
    order_own = deal_order(position)
    order_other = deal_order(sorted_positions(other_owners))
    wanted = jnp.arange(PART_SHOTS, dtype=jnp.int32) * 8 + group
    mine = wanted[:, None] == position[None, :]
    part_map = jnp.sum(jnp.where(mine[:, :, None], trace_map[None], 0), axis=1)
    part_owner = jnp.sum(jnp.where(mine, owners[None, :], 0), axis=1)
    key = part_owner[:, None] * TIMES + jnp.arange(TIMES, dtype=jnp.int32)[None, :]
    key = key.reshape(1, PART_SHOTS * TIMES)
    line = jnp.arange(OWNERS * TIMES, dtype=jnp.int32)[:, None]
    spread = (line == key).astype(BF)
    swapped = (line == key + 4 - 8 * ((key // 4) % 2)).astype(BF)

    estimate = scale(place, wavelet, keep, came, order_own, order_other)
    spectra = lax.all_to_all(estimate, FREQ_AXES + ("xl",), 0, 0, tiled=True)
    turns = turn_matrices(near_owners, sources, me)
    rows = transform(spectra, part_map, spread, swapped).reshape(256, 16, 128)
    arrived = lax.all_to_all(rows, SHOT_AXES + FREQ_AXES, 0, 0, tiled=True)
    return place_rows(arrived, turns)


def solution(mesh):
    fine = Mesh(mesh.devices.reshape(2, 8, 2, 2, 4), SHOT_AXES + FREQ_AXES)
    placed = (
        P(None, FREQ_AXES, SHOT_AXES, None),
        P(None, FREQ_AXES),
        P(SHOT_AXES, None),
        P(SHOT_AXES, None),
    )
    return jax.shard_map(
        shards,
        mesh=fine,
        in_specs=placed,
        out_specs=P(FREQ_AXES, SHOT_AXES, None),
        check_vma=False,
    )
```

```python
import jax
import jax.numpy as jnp
import numpy as np
from jax import lax
from jax.experimental import pallas as pl
from jax.experimental.pallas import tpu as pltpu
from jax.sharding import Mesh, PartitionSpec as P

SHOTS = 128
WINDOW = 512
FREQS = 16
TIMES = 32
OWNERS = 32
PART_SHOTS = 16
DEPTH = 8
SHOT_AXES = ("xl", "z", "core")
FREQ_AXES = ("xh", "y")
BF = jnp.bfloat16
F32 = jnp.float32
PARAMS = pltpu.CompilerParams(vmem_limit_bytes=48 * 1024 * 1024)


def dot(a, b):
    return jnp.dot(a, b, preferred_element_type=F32)


def transform_tables():
    f = np.arange(FREQS)[None, :]
    t = np.arange(TIMES)[:, None]
    angle = ((f + 1) * t) % (2 * FREQS) * (np.pi / FREQS)
    table = np.stack([np.cos(angle), -np.sin(angle)], axis=2) / FREQS
    table = table.reshape(TIMES, 2 * FREQS)
    full = np.einsum("tq,ab->atqb", table, np.eye(PART_SHOTS))
    full = full.reshape(PART_SHOTS * TIMES, 2 * FREQS * PART_SHOTS).astype(np.float32)
    high = full.astype(BF)
    low = (full - high.astype(np.float32)).astype(BF)
    return np.concatenate([high, low], axis=0)


HBM = pl.BlockSpec(memory_space=pltpu.HBM)
ANY = pl.BlockSpec(memory_space=pl.ANY)
SMEM = pl.BlockSpec(memory_space=pltpu.SMEM)
CHUNK = 1024
STRIP = 16


def run_copies(pairs, sems):
    copies = [
        pltpu.make_async_copy(source, target, sems.at[n])
        for n, (source, target) in enumerate(pairs)
    ]
    for copy in copies:
        copy.start()
    return copies


def window_kernel(place, wave, strip, own, give, sems):
    pairs = []
    for target, freq in ((own, place[0]), (give, 1 - place[0])):
        for part in range(2):
            for column in range(4):
                pairs.append(
                    (
                        wave.at[part, freq, :, pl.ds(column * 128, 128)],
                        target.at[pl.ds((part * 4 + column) * 128, 128), :],
                    )
                )
        pairs.append((strip, target.at[pl.ds(CHUNK, STRIP), :]))
    for copy in run_copies(pairs, sems):
        copy.wait()


def window_chunks(place, wavefield, strip):
    return pl.pallas_call(
        window_kernel,
        out_shape=[jax.ShapeDtypeStruct((CHUNK + STRIP, 128), BF)] * 2,
        in_specs=[SMEM, HBM, ANY],
        out_specs=[ANY] * 2,
        scratch_shapes=[pltpu.SemaphoreType.DMA((18,))],
        compiler_params=PARAMS,
    )(place, wavefield, strip)


def halves_kernel(place, wave, diag, same, partner, far, near, sems):
    xl, core = place[0], place[1]
    copies = run_copies(
        [
            (wave.at[0, 1 - xl, :, pl.ds(WINDOW, 3584)], far.at[0]),
            (wave.at[1, 1 - xl, :, pl.ds(WINDOW, 3584)], far.at[1]),
            (wave.at[0, xl], near.at[0]),
            (wave.at[1, xl], near.at[1]),
        ],
        sems,
    )
    for n, copy in enumerate(copies):
        copy.wait()
        part = n % 2
        here = far if n < 2 else near
        for block in range(14 if n < 2 else 16):
            a = here[part, :, block * 256 : block * 256 + 128]
            b = here[part, :, block * 256 + 128 : block * 256 + 256]
            target = slice(block * 128, block * 128 + 128)
            if n < 2:
                same[part, :, target] = jnp.where(core == 0, a, b)
                diag[part, :, target] = jnp.where(core == 0, b, a)
            else:
                partner[part, :, target] = jnp.where(core == 0, b, a)


def column_halves(place, wavefield):
    return pl.pallas_call(
        halves_kernel,
        out_shape=[
            jax.ShapeDtypeStruct((2, SHOTS, 1792), BF),
            jax.ShapeDtypeStruct((2, SHOTS, 1792), BF),
            jax.ShapeDtypeStruct((2, SHOTS, 2048), BF),
        ],
        in_specs=[SMEM, HBM],
        scratch_shapes=[
            pltpu.VMEM((2, SHOTS, 3584), BF),
            pltpu.VMEM((2, SHOTS, 4096), BF),
            pltpu.SemaphoreType.DMA((4,)),
        ],
        compiler_params=PARAMS,
    )(place, wavefield)


def follow_kernel(value, earlier, out):
    pass


def follow(value, earlier, flops=0):
    return pl.pallas_call(
        follow_kernel,
        cost_estimate=pl.CostEstimate(flops=flops, bytes_accessed=flops // 500, transcendentals=0),
        out_shape=jax.ShapeDtypeStruct(value.shape, value.dtype),
        in_specs=[pl.BlockSpec(memory_space=pl.ANY)] * 2,
        out_specs=pl.BlockSpec(memory_space=pl.ANY),
        input_output_aliases={0: 0},
    )(value, earlier)


def pick(place, block, refs, part):
    if len(refs) == 1:
        return refs[0][part, :, pl.ds(pl.multiple_of(block * 128, 128), 128)]
    rest, window = refs
    late = jnp.maximum(block - 2, 0)
    early = jnp.minimum(block, 1) * 2 + place[1]
    a = rest[part, :, pl.ds(pl.multiple_of(late * 128, 128), 128)]
    b = window[pl.ds(pl.multiple_of((part * 4 + early) * 128, 128), 128), :]
    return jnp.where(block < 2, b, a)


def window_columns(chunk, part):
    return jnp.concatenate(
        [chunk[(part * 4 + n) * 128 : (part * 4 + n + 1) * 128, :] for n in range(4)], axis=1
    )


def multiply(place, rows, near, far, depth):
    xl = place[0]
    sides = []
    for part in range(2):
        lines = []
        for refs in rows:
            a = pick(place, xl * DEPTH + depth, refs, part)
            b = pick(place, (1 - xl) * DEPTH + depth, refs, part)
            lines.append(jnp.concatenate([a, b], axis=1))
        sides.append(jnp.concatenate(lines, axis=0))
    ar, ai = sides
    lines = jnp.concatenate([ar, -ai], axis=1), jnp.concatenate([ai, ar], axis=1)
    columns = [window_columns(chunk, part) for part in range(2) for chunk in (near, far)]
    return dot(jnp.concatenate(lines, axis=0), jnp.concatenate(columns, axis=0))


def product(place, wavefield, line, other_line, near, far):
    distances = list(far)
    count = len(distances)
    size = 2 * SHOTS
    rest, window = other_line

    def kernel(place, line_in, rest_in, window_in, *refs):
        near_in, far_in = refs[:count], refs[count : 2 * count]
        out, total, near_here, far_here, line_here, rest_here, window_here, sems = refs[2 * count :]
        pairs = [(rest_in, rest_here), (window_in.at[pl.ds(0, CHUNK), :], window_here)]
        if line is None:
            for block in range(16):
                column = pl.multiple_of((2 * block + place[1]) * 128, 128)
                pairs.append(
                    (
                        line_in.at[:, place[0], :, pl.ds(column, 128)],
                        line_here.at[:, :, pl.ds(block * 128, 128)],
                    )
                )
        else:
            pairs.append((line_in, line_here))
        first = len(pairs)
        for n in range(count):
            pairs.append((near_in[n].at[pl.ds(0, CHUNK), :], near_here.at[n]))
            pairs.append((far_in[n].at[pl.ds(0, CHUNK), :], far_here.at[n]))
        copies = run_copies(pairs, sems)
        for copy in copies[:first]:
            copy.wait()
        groups = [(line_here,), (rest_here, window_here)]
        for n in range(count):
            copies[first + 2 * n].wait()
            copies[first + 2 * n + 1].wait()
            depth = lax.rem(place[2] - distances[n] + 2 * DEPTH, DEPTH)
            value = multiply(place, groups, near_here.at[n], far_here.at[n], depth)
            if n == 0:
                total[...] = value
            elif n < count - 1:
                total[...] += value
            else:
                out[0] = (total[:size] + value[:size]).astype(out.dtype)
                out[1] = (total[size:] + value[size:]).astype(out.dtype)

    return pl.pallas_call(
        kernel,
        out_shape=jax.ShapeDtypeStruct((2, size, WINDOW), BF if line is None else F32),
        in_specs=[SMEM, HBM if line is None else ANY] + [ANY] * (2 + 2 * count),
        scratch_shapes=[
            pltpu.VMEM((2 * size, WINDOW), F32),
            pltpu.VMEM((count, CHUNK, 128), BF),
            pltpu.VMEM((count, CHUNK, 128), BF),
            pltpu.VMEM((2, SHOTS, 2048), BF),
            pltpu.VMEM(rest.shape, BF),
            pltpu.VMEM((CHUNK, 128), BF),
            pltpu.SemaphoreType.DMA((18 + 2 * count,)),
        ],
        compiler_params=PARAMS,
        cost_estimate=pl.CostEstimate(
            flops=2 * size * 512 * 1024 * count, bytes_accessed=2**22, transcendentals=0
        ),
    )(
        place,
        wavefield if line is None else line,
        rest,
        window,
        *[near[d] for d in distances],
        *[far[d] for d in distances],
    )


def scale_kernel(place, wave, keep, came, order_own, order_other, out):
    xl = place[0]
    wr = wave[0, xl]
    wi = wave[1, xl]
    for block in range(2):
        where = xl if block == 0 else 1 - xl
        order = order_own[...] if block == 0 else order_other[...]
        rows = slice(block * SHOTS, (block + 1) * SHOTS)
        real = keep[0, rows].astype(F32) + came[0, rows]
        imag = keep[1, rows].astype(F32) + came[1, rows]
        er = (real * wr - imag * wi).astype(BF)
        ei = (real * wi + imag * wr).astype(BF)
        sr = dot(order, er).astype(BF)
        si = dot(order, ei).astype(BF)
        for part in range(8):
            some = slice(part * PART_SHOTS, (part + 1) * PART_SHOTS)
            out[2 * part + where, 0:16, :] = sr[some]
            out[2 * part + where, 16:32, :] = si[some]


def scale(place, wavelet, keep, came, order_own, order_other):
    return pl.pallas_call(
        scale_kernel,
        out_shape=jax.ShapeDtypeStruct((16, 32, WINDOW), BF),
        in_specs=[pl.BlockSpec(memory_space=pltpu.SMEM)] * 2
        + [pl.BlockSpec(memory_space=pltpu.VMEM)] * 4,
        compiler_params=PARAMS,
    )(place, wavelet, keep, came, order_own, order_other)


def transform_kernel(spectra, tables, trace_map, spread, swapped, out, traces, moved):
    x = spectra[...].reshape(512, WINDOW)
    both = dot(tables[...], x)
    traces[...] = (both[:512] + both[512:]).astype(BF)
    receivers = lax.broadcasted_iota(jnp.int32, (WINDOW, WINDOW), 0)
    for shot in range(PART_SHOTS):
        rows = slice(shot * TIMES, (shot + 1) * TIMES)
        chosen = jnp.where(receivers == trace_map[shot : shot + 1, :], 1.0, 0.0).astype(BF)
        moved[rows, :] = dot(traces[rows, :], chosen).astype(BF)
    upper = lax.broadcasted_iota(jnp.int32, (128, 8, 128), 1) < 4
    even, odd = [], []
    for pair in range(2):
        first = slice(pair * 256, pair * 256 + 128)
        second = slice(pair * 256 + 128, pair * 256 + 256)
        both = moved[:, pair * 256 : (pair + 1) * 256]
        plain = dot(spread[...], both).reshape(128, 8, 256)
        other = dot(swapped[...], both).reshape(128, 8, 256)
        even.append(jnp.where(upper, plain[..., :128], other[..., 128:]))
        odd.append(jnp.where(upper, other[..., :128], plain[..., 128:]))
    out[:, 0] = jnp.concatenate(even, axis=1).astype(BF)
    out[:, 1] = jnp.concatenate(odd, axis=1).astype(BF)


def transform(spectra, trace_map, spread, swapped):
    return pl.pallas_call(
        transform_kernel,
        out_shape=jax.ShapeDtypeStruct((128, 2, 16, 128), BF),
        scratch_shapes=[pltpu.VMEM((512, WINDOW), BF)] * 2,
        compiler_params=PARAMS,
    )(spectra, jnp.asarray(transform_tables()), trace_map, spread, swapped)


def place_kernel(arrived, turns, out):
    for pair in range(16):
        block = arrived[pair * 16 : (pair + 1) * 16].reshape(256, 128)
        turned = dot(turns[pair], block).astype(BF)
        for column in range(4):
            for time in range(4):
                first = (column * 4 + time) * 16
                out[time, pair * 16 : (pair + 1) * 16, column * 128 : (column + 1) * 128] = (
                    turned[first : first + 16]
                )


def place_rows(arrived, turns):
    return pl.pallas_call(
        place_kernel,
        out_shape=jax.ShapeDtypeStruct((4, OWNERS * 8, WINDOW), BF),
        compiler_params=PARAMS,
    )(arrived, turns)


def sorted_positions(owners):
    shot = jnp.arange(SHOTS, dtype=jnp.int32)
    less = owners[None, :] < owners[:, None]
    same = (owners[None, :] == owners[:, None]) & (shot[None, :] < shot[:, None])
    return jnp.sum((less | same).astype(jnp.int32), axis=1)


def deal_order(position):
    row = jnp.arange(SHOTS, dtype=jnp.int32)
    wanted = (row % PART_SHOTS) * 8 + row // PART_SHOTS
    return (wanted[:, None] == position[None, :]).astype(BF)


def turn_matrices(near_owners, sources, me):
    number = jnp.arange(OWNERS, dtype=jnp.int32)
    before = jnp.sum((near_owners < me).astype(jnp.int32), axis=1)
    start = jnp.sum(
        jnp.where(number[:, None] == sources[None, :], before[None, :], 0), axis=1
    )
    group = jnp.arange(8, dtype=jnp.int32)
    rank = (group[None, :] - start[:, None] + SHOTS) % 8
    rank = rank.reshape(16, 2, 8, 1, 1)
    source = jnp.arange(2, dtype=jnp.int32).reshape(1, 2, 1, 1, 1)
    column = jnp.arange(4, dtype=jnp.int32).reshape(1, 1, 1, 4, 1)
    time = jnp.arange(4, dtype=jnp.int32).reshape(1, 1, 1, 1, 4)
    key = (column * 64 + time * 16 + source * 8 + rank).reshape(16, 1, 256)
    return (jnp.arange(256, dtype=jnp.int32)[None, :, None] == key).astype(BF)


def shards(wavefield, wavelet, shot_owner, trace_map):
    xl = lax.axis_index("xl")
    core = lax.axis_index("core")
    depth = lax.axis_index("z")
    group = lax.axis_index(FREQ_AXES)
    me = lax.axis_index(SHOT_AXES)
    swap = [(0, 1), (1, 0)]
    cross = [(n, 3 - n) for n in range(4)]
    right = [(n, (n + 1) % DEPTH) for n in range(DEPTH)]
    left = [(n, (n - 1) % DEPTH) for n in range(DEPTH)]
    place = jnp.stack([xl, core, depth]).astype(jnp.int32)

    owners = shot_owner[:, 0]
    strip = jnp.broadcast_to(owners.astype(BF)[None], (STRIP, SHOTS))
    own_window, give_window = window_chunks(place, wavefield, strip)
    xw = lax.ppermute(give_window, "xl", swap)
    diag, same, partner = column_halves(place, wavefield)
    diag = lax.ppermute(diag, ("xl", "core"), cross)
    partner = lax.ppermute(partner, "core", swap)
    same = lax.ppermute(follow(same, diag, 3 * 10**10), "xl", swap)
    xpw = lax.ppermute(xw, "core", swap)
    near = {0: own_window}
    far = {0: xw}
    for step in range(1, 5):
        near[step] = lax.ppermute(near[step - 1], "z", right)
        far[-step] = lax.ppermute(far[1 - step], "z", left)
        if step < 4:
            near[-step] = lax.ppermute(near[1 - step], "z", left)
            far[step] = lax.ppermute(far[step - 1], "z", right)
    far[4] = far.pop(-4)
    send = product(place, wavefield, partner, (diag, xpw), near, far)
    came = lax.ppermute(send, "core", swap)
    keep = product(place, wavefield, None, (same, xw), near, far)

    other_owners = xw[CHUNK].astype(jnp.int32)
    distances = list(far)
    strips = [near[d][CHUNK : CHUNK + 1] for d in distances]
    strips += [far[d][CHUNK : CHUNK + 1] for d in distances]
    strips = jnp.concatenate(strips, axis=0)
    near_owners = jnp.concatenate([strips, lax.ppermute(strips, "core", swap)], axis=0)
    near_owners = near_owners.astype(jnp.int32)
    depths = (depth - jnp.asarray(distances, dtype=jnp.int32) + DEPTH) % DEPTH * 2
    sources = jnp.concatenate([depths + 16 * xl, depths + 16 * (1 - xl)])
    sources = jnp.concatenate([sources + core, sources + 1 - core])
    position = sorted_positions(owners)
    order_own = deal_order(position)
    order_other = deal_order(sorted_positions(other_owners))
    wanted = jnp.arange(PART_SHOTS, dtype=jnp.int32) * 8 + group
    mine = wanted[:, None] == position[None, :]
    part_map = jnp.sum(jnp.where(mine[:, :, None], trace_map[None], 0), axis=1)
    part_owner = jnp.sum(jnp.where(mine, owners[None, :], 0), axis=1)
    key = part_owner[:, None] * TIMES + jnp.arange(TIMES, dtype=jnp.int32)[None, :]
    key = key.reshape(1, PART_SHOTS * TIMES)
    line = jnp.arange(OWNERS * TIMES, dtype=jnp.int32)[:, None]
    spread = (line == key).astype(BF)
    swapped = (line == key + 4 - 8 * ((key // 4) % 2)).astype(BF)

    estimate = scale(place, wavelet, keep, came, order_own, order_other)
    spectra = lax.all_to_all(estimate, FREQ_AXES + ("xl",), 0, 0, tiled=True)
    turns = turn_matrices(near_owners, sources, me)
    rows = transform(spectra, part_map, spread, swapped).reshape(256, 16, 128)
    arrived = lax.all_to_all(rows, SHOT_AXES + FREQ_AXES, 0, 0, tiled=True)
    return place_rows(arrived, turns)


def solution(mesh):
    fine = Mesh(mesh.devices.reshape(2, 8, 2, 2, 4), SHOT_AXES + FREQ_AXES)
    placed = (
        P(None, FREQ_AXES, SHOT_AXES, None),
        P(None, FREQ_AXES),
        P(SHOT_AXES, None),
        P(SHOT_AXES, None),
    )
    return jax.shard_map(
        shards,
        mesh=fine,
        in_specs=placed,
        out_specs=P(FREQ_AXES, SHOT_AXES, None),
        check_vma=False,
    )
```
